512 devices in a mesh: grp: 32 (over x, z_hi, core), leaf: 16 (over y, z_lo).
Axes of the slice: x: 4, y: 4, z: 16 (z_hi: 4, z_lo: 4; z = z_hi * 4 + z_lo), core: 2. Of those that a mesh axis runs over, the one named last changes fastest.
Arguments:
- charges: bfloat16 [64, 524288], P(None, ('grp', 'leaf')), may hold values from -6 to 6
- interp_basis: bfloat16 [2048, 256, 128], P(('grp', 'leaf')), may hold values from -0.375 to 0.375
- coupling: bfloat16 [4, 2048, 2, 128, 128], P(None, ('grp', 'leaf')), may hold values from -0.5 to 0.5
- expand_basis: bfloat16 [2048, 128, 256], P(('grp', 'leaf')), may hold values from -0.5 to 0.5
- block_rank: int32 [5, 2048], P(None, ('grp', 'leaf')), may hold values from 64 to 128
- leaf_partner: int32 [2048], P(('grp', 'leaf')), may hold values from 0 to 2047, as said below
Outputs:
- potential: bfloat16 [64, 524288], P(None, ('grp', 'leaf'))
The draws below stay inside these ranges and needn't reach their ends.
Inputs may be any that keep to these rules, and one draw needn't show every extreme that they name: leaf_partner is a permutation of the blocks that maps every aligned run of 64 blocks onto itself.
All inputs are finite; a program needn't handle non-finite values.
Results may differ from the reference program's by a relative error of at most 0.0075.
Values may be sent and summed in bfloat16 or wider, within the bound.
A program may use at most 64 MiB of HBM per device.

```python
import jax
import jax.numpy as jnp

K = 128
M = 256
R = 64
BD = 4
LEVELS = 3
GROUPB = 64
NB = 2048
ROWS = 524288
N_GRP = 32
N_LEAF = 16


def draw_leaf_partner(key, part):
    key = jax.random.fold_in(key, 11)
    keys = jax.random.split(key, N_GRP * N_LEAF * BD // GROUPB)
    perms = jax.vmap(lambda sub: jax.random.permutation(sub, GROUPB))(keys).astype(jnp.int32)
    offsets = (jnp.arange(perms.shape[0], dtype=jnp.int32) * GROUPB)[:, None]
    return (perms + offsets).reshape(-1)


def with_ends(drawn, own_key, least, largest):
    index_at = [jax.random.randint(jax.random.fold_in(own_key, axis), (), 0, length) for axis, length in enumerate(drawn.shape)]
    main_axis = drawn.shape.index(max(drawn.shape))
    neighbour = index_at[:main_axis] + [(index_at[main_axis] + 1) % drawn.shape[main_axis]] + index_at[main_axis + 1:]
    return drawn.at[tuple(index_at)].set(least).at[tuple(neighbour)].set(largest)


def block_scale(key, shape, cuts, smallest, high):
    level = 1.0
    for position, blocks in cuts:
        steps = jax.random.uniform(jax.random.fold_in(jax.random.fold_in(key, 6), position), (blocks,), jnp.float32, smallest / len(cuts), high / len(cuts))
        level = level * jnp.repeat(jnp.exp(steps), shape[position] // blocks).reshape((-1,) + (1,) * (len(shape) - 1 - position))
    return level


def scatter_about(stream_key, shape, scale, most, cuts=(), kind=jnp.bfloat16):
    values = scale * jax.random.normal(stream_key, shape, jnp.float32)
    if cuts:
        values = values * block_scale(stream_key, shape, cuts, -0.22, 0.18)
    return jnp.clip(values, -most, most).astype(kind)


def setup_inputs(seed: int = 0) -> dict:
    key_of = jax.random.split(jax.random.key(seed), 7)
    return {
        "charges": scatter_about(key_of[0], (R, ROWS), 1.0, 6.0, ((1, 512),)),
        "interp_basis": scatter_about(key_of[1], (NB, M, K), M ** -0.5, 0.375, ((0, 512),)),
        "coupling": scatter_about(key_of[2], (LEVELS + 1, NB, 2, K, K), K ** -0.5, 0.5, ((1, 512),)),
        "expand_basis": scatter_about(key_of[3], (NB, K, M), K ** -0.5, 0.5, ((0, 512),)),
        "block_rank": with_ends(jax.random.randint(key_of[4], (LEVELS + 2, NB), K // 2, K + 1), jax.random.fold_in(key_of[4], 1), K // 2, K).astype(jnp.int32),
        "leaf_partner": draw_leaf_partner(jax.random.fold_in(key_of[6], 71), 0),
    }


def masked(values, ranks):
    cols = jnp.arange(values.shape[-1], dtype=jnp.int32)
    keep = (cols[None, None, :] < ranks[:, None, None]).astype(jnp.float32)
    return values * keep


def apply_pair(own, other, factors, ranks):
    first = jnp.einsum("jrk,jkq->jrq", own.astype(jnp.float32), factors[:, 0].astype(jnp.float32))
    second = jnp.einsum("jrk,jkq->jrq", other.astype(jnp.float32), factors[:, 1].astype(jnp.float32))
    return masked(first + second, ranks).astype(jnp.bfloat16)


def reference(charges, interp_basis, coupling, expand_basis, block_rank, leaf_partner):
    blocks = interp_basis.shape[0]
    size_m = interp_basis.shape[1]
    grouped = charges.reshape(charges.shape[0], blocks, size_m).astype(jnp.float32)
    compressed = jnp.einsum("rjm,jmk->jrk", grouped, interp_basis.astype(jnp.float32))
    compressed = masked(compressed, block_rank[0]).astype(jnp.bfloat16)
    state = apply_pair(compressed, compressed[leaf_partner], coupling[0], block_rank[1])
    grp_bits = N_GRP.bit_length() - 1
    index = jnp.arange(blocks, dtype=jnp.int32)
    for level in range(LEVELS):
        bit = ((level + 1) * grp_bits) // LEVELS - 1
        stride = (1 << bit) * GROUPB
        partner = jnp.bitwise_xor(index, stride)
        state = apply_pair(state, state[partner], coupling[level + 1], block_rank[level + 2])
    result = jnp.einsum("jrk,jkm->rjm", state.astype(jnp.float32), expand_basis.astype(jnp.float32))
    return result.reshape(charges.shape[0], blocks * size_m).astype(jnp.bfloat16)
```

```python
import jax
import jax.numpy as jnp
from jax import lax
from jax.experimental import pallas as pl
from jax.experimental.pallas import tpu as pltpu
from jax.sharding import PartitionSpec as P

LEVELS = 3
MESH = pl.DeviceIdType.MESH


def kernel(
    charges_hbm, interp_hbm, coupling_hbm, expand_hbm, rank_ref, partner_ref, out_hbm,
    charges, interp, coupling, expand, out, subtree, state, other,
    load_sems, gather_send, gather_recv, level_send, level_recv, out_sems,
):
    grp, leaf = lax.axis_index("grp"), lax.axis_index("leaf")
    n_leaf = lax.axis_size("leaf")
    grp_bits = lax.axis_size("grp").bit_length() - 1
    blocks, size_m, rank = interp.shape
    rows = charges.shape[0]

    mates = [lax.rem(leaf + step, n_leaf) for step in range(1, n_leaf)]
    pairs = []
    for level in range(LEVELS):
        stride = 1 << ((level + 1) * grp_bits // LEVELS - 1)
        pairs.append(grp + stride * (1 - 2 * lax.rem(grp // stride, 2)))
    barrier = pltpu.get_barrier_semaphore()
    for pair in pairs:
        pl.semaphore_signal(barrier, inc=1, device_id=(pair, leaf), device_id_type=MESH)
    for mate in mates:
        pl.semaphore_signal(barrier, inc=1, device_id=(grp, mate), device_id_type=MESH)

    loads = [
        pltpu.make_async_copy(src, dst, load_sems.at[i])
        for i, (src, dst) in enumerate(
            ((charges_hbm, charges), (interp_hbm, interp), (coupling_hbm, coupling), (expand_hbm, expand))
        )
    ]
    for load in loads:
        load.start()

    cols = lax.broadcasted_iota(jnp.int32, (rows, rank), 1)

    def keep(section, block, values):
        return jnp.where(cols < rank_ref[section, block], values, 0.0).astype(jnp.bfloat16)

    def dot(a, b):
        return jnp.dot(a, b, preferred_element_type=jnp.float32)

    loads[0].wait()
    loads[1].wait()
    for block in range(blocks):
        made = dot(charges[:, pl.ds(block * size_m, size_m)], interp[block])
        subtree[leaf * blocks + block] = keep(0, block, made)

    pl.semaphore_wait(barrier, len(mates) + len(pairs))
    mine = subtree.at[pl.ds(leaf * blocks, blocks)]
    sends = []
    for step, mate in enumerate(mates):
        send = pltpu.make_async_remote_copy(
            src_ref=mine, dst_ref=mine, send_sem=gather_send.at[step], recv_sem=gather_recv.at[step],
            device_id=(grp, mate), device_id_type=MESH,
        )
        send.start()
        sends.append(send)

    loads[2].wait()
    own = [dot(subtree[leaf * blocks + block], coupling[0, block, 0]) for block in range(blocks)]
    for send in sends:
        send.wait_recv()
    for block in range(blocks):
        picked = subtree[lax.rem(partner_ref[block], blocks * n_leaf)]
        state[0, block] = keep(1, block, own[block] + dot(picked, coupling[0, block, 1]))

    for level in range(LEVELS):
        swap = pltpu.make_async_remote_copy(
            src_ref=state.at[level], dst_ref=other.at[level],
            send_sem=level_send.at[level], recv_sem=level_recv.at[level],
            device_id=(pairs[level], leaf), device_id_type=MESH,
        )
        swap.start()
        sends.append(swap)
        own = [dot(state[level, block], coupling[level + 1, block, 0]) for block in range(blocks)]
        swap.wait_recv()
        for block in range(blocks):
            total = own[block] + dot(other[level, block], coupling[level + 1, block, 1])
            state[level + 1, block] = keep(level + 2, block, total)

    loads[3].wait()
    stores = []
    for block in range(blocks):
        part = pl.ds(block * size_m, size_m)
        out[:, part] = dot(state[LEVELS, block], expand[block]).astype(jnp.bfloat16)
        store = pltpu.make_async_copy(out.at[:, part], out_hbm.at[:, part], out_sems.at[block])
        store.start()
        stores.append(store)
    for send in sends:
        send.wait_send()
    for store in stores:
        store.wait()


def shards(charges, interp_basis, coupling, expand_basis, block_rank, leaf_partner):
    n_leaf = lax.axis_size("leaf")
    blocks, size_m, rank = interp_basis.shape
    rows = charges.shape[0]
    any_spec = pl.BlockSpec(memory_space=pl.ANY)
    smem_spec = pl.BlockSpec(memory_space=pltpu.SMEM)
    bf16 = jnp.bfloat16
    return pl.pallas_call(
        kernel,
        out_shape=jax.ShapeDtypeStruct(charges.shape, bf16),
        in_specs=[any_spec] * 4 + [smem_spec] * 2,
        out_specs=any_spec,
        scratch_shapes=[
            pltpu.VMEM(charges.shape, bf16),
            pltpu.VMEM(interp_basis.shape, bf16),
            pltpu.VMEM(coupling.shape, bf16),
            pltpu.VMEM(expand_basis.shape, bf16),
            pltpu.VMEM(charges.shape, bf16),
            pltpu.VMEM((n_leaf * blocks, rows, rank), bf16),
            pltpu.VMEM((LEVELS + 1, blocks, rows, rank), bf16),
            pltpu.VMEM((LEVELS, blocks, rows, rank), bf16),
            pltpu.SemaphoreType.DMA((4,)),
            pltpu.SemaphoreType.DMA((n_leaf - 1,)),
            pltpu.SemaphoreType.DMA((n_leaf - 1,)),
            pltpu.SemaphoreType.DMA((LEVELS,)),
            pltpu.SemaphoreType.DMA((LEVELS,)),
            pltpu.SemaphoreType.DMA((blocks,)),
        ],
        compiler_params=pltpu.CompilerParams(
            collective_id=0, has_side_effects=True, vmem_limit_bytes=60 * 1024 * 1024
        ),
    )(charges, interp_basis, coupling, expand_basis, block_rank, leaf_partner)


def solution(mesh):
    in_specs = (
        P(None, ("grp", "leaf")),
        P(("grp", "leaf"), None, None),
        P(None, ("grp", "leaf"), None, None, None),
        P(("grp", "leaf"), None, None),
        P(None, ("grp", "leaf")),
        P(("grp", "leaf")),
    )
    out_specs = P(None, ("grp", "leaf"))
    return jax.shard_map(shards, mesh=mesh, in_specs=in_specs, out_specs=out_specs, check_vma=False)
```

```python
import math

import jax
import jax.numpy as jnp
from jax import lax
from jax.experimental import pallas as pl
from jax.experimental.pallas import tpu as pltpu
from jax.sharding import PartitionSpec as P

LEVELS = 3
MESH = pl.DeviceIdType.MESH


def kernel(
    charges_hbm, interp_hbm, coupling_hbm, expand_hbm, rank_ref, partner_ref, out_hbm,
    charges, interp, coupling, expand, out, wanted, near_y, near_z, picked, found_z, found_y, state, other,
    load_sems, ask_send, ask_recv, near_send, near_recv, far_send, far_recv,
    level_send, level_recv, out_sems,
):
    grp, leaf = lax.axis_index("grp"), lax.axis_index("leaf")
    n_leaf = lax.axis_size("leaf")
    near, found = (near_y, near_z), (found_z, found_y)
    side = near_y.shape[0]
    grp_bits = lax.axis_size("grp").bit_length() - 1
    blocks, size_m, rank = interp.shape
    rows = charges.shape[0]
    half = rows // 2

    place = (leaf // side, lax.rem(leaf, side))

    def peer(axis, step):
        at = lax.rem(place[axis] + step, side)
        return at, (at * side + place[1] if axis == 0 else place[0] * side + at)

    pairs = []
    for level in range(LEVELS):
        stride = 1 << ((level + 1) * grp_bits // LEVELS - 1)
        pairs.append(grp + stride * (1 - 2 * lax.rem(grp // stride, 2)))
    barrier = pltpu.get_barrier_semaphore()
    for pair in pairs:
        pl.semaphore_signal(barrier, inc=1, device_id=(pair, leaf), device_id_type=MESH)
    for axis in range(2):
        for step in range(1, side):
            pl.semaphore_signal(
                barrier, inc=1, device_id=(grp, peer(axis, step)[1]), device_id_type=MESH
            )

    loads = [
        pltpu.make_async_copy(src, dst, load_sems.at[i])
        for i, (src, dst) in enumerate(
            ((charges_hbm, charges), (interp_hbm, interp), (coupling_hbm, coupling), (expand_hbm, expand))
        )
    ]
    for load in loads:
        load.start()

    def remote(src, dst, send_sem, recv_sem, device):
        return pltpu.make_async_remote_copy(
            src_ref=src, dst_ref=dst, send_sem=send_sem, recv_sem=recv_sem,
            device_id=device, device_id_type=MESH,
        )

    cols = lax.broadcasted_iota(jnp.int32, (rows, rank), 1)

    def keep(section, block, values):
        mask = cols[: values.shape[0]] < rank_ref[block, section]
        return jnp.where(mask, values, 0.0).astype(jnp.bfloat16)

    def dot(a, b):
        return jnp.dot(a, b, preferred_element_type=jnp.float32)

    loads[0].wait()
    loads[1].wait()
    leaves = []
    for block in range(blocks):
        made = keep(0, block, dot(charges[:, pl.ds(block * size_m, size_m)], interp[block]))
        leaves.append(made)
        for h in range(2):
            near[h][place[h], block] = made[h * half : (h + 1) * half]

    pl.semaphore_wait(barrier, 2 * (side - 1) + LEVELS)
    asks, nears, fars = [], [], []
    for h in range(2):
        for step in range(1, side):
            k = h * (side - 1) + step - 1
            first, second = peer(h, step), peer(1 - h, step)
            ask = remote(
                partner_ref, wanted.at[h, place[1 - h]], ask_send.at[k], ask_recv.at[k], (grp, second[1])
            )
            ask.start()
            asks.append(ask)
            mine = near[h].at[place[h]]
            send = remote(mine, mine, near_send.at[k], near_recv.at[k], (grp, first[1]))
            send.start()
            nears.append(send)

    loads[2].wait()
    own = [dot(leaves[block], coupling[0, block, 0]) for block in range(blocks)]
    for ask in asks:
        ask.wait_recv()

    def origin(value):
        at = lax.rem(value, blocks * n_leaf)
        device, block = at // blocks, lax.rem(at, blocks)
        return (device // side, lax.rem(device, side)), block

    for h in range(2):
        for step in range(1, side):
            nears[h * (side - 1) + step - 1].wait_recv()
        for step in range(1, side):
            k = h * (side - 1) + step - 1
            at, device = peer(1 - h, step)
            for block in range(blocks):
                source, index = origin(wanted[h, at, block])
                picked[h, step - 1, block] = near[h][source[h], index]
            send = remote(
                picked.at[h, step - 1], found[h].at[place[1 - h]], far_send.at[k], far_recv.at[k], (grp, device)
            )
            send.start()
            fars.append(send)
        for block in range(blocks):
            source, index = origin(partner_ref[block])
            found[h][place[1 - h], block] = near[h][source[h], index]
    for far in fars:
        far.wait_recv()
    for block in range(blocks):
        source, _ = origin(partner_ref[block])
        for h in range(2):
            total = dot(found[h][source[1 - h], block], coupling[0, block, 1])
            part = slice(h * half, (h + 1) * half)
            state[0, block, part] = keep(1, block, own[block][part] + total)

    sends = asks + nears + fars
    for level in range(LEVELS):
        swap = remote(
            state.at[level], other.at[level], level_send.at[level], level_recv.at[level], (pairs[level], leaf)
        )
        swap.start()
        sends.append(swap)
        own = [dot(state[level, block], coupling[level + 1, block, 0]) for block in range(blocks)]
        swap.wait_recv()
        for block in range(blocks):
            total = own[block] + dot(other[level, block], coupling[level + 1, block, 1])
            state[level + 1, block] = keep(level + 2, block, total)

    loads[3].wait()
    stores = []
    for block in range(blocks):
        part = pl.ds(block * size_m, size_m)
        out[:, part] = dot(state[LEVELS, block], expand[block]).astype(jnp.bfloat16)
        store = pltpu.make_async_copy(out.at[:, part], out_hbm.at[:, part], out_sems.at[block])
        store.start()
        stores.append(store)
    for send in sends:
        send.wait_send()
    for store in stores:
        store.wait()


def shards(charges, interp_basis, coupling, expand_basis, block_rank, leaf_partner):
    side = math.isqrt(lax.axis_size("leaf"))
    blocks, size_m, rank = interp_basis.shape
    rows = charges.shape[0]
    any_spec = pl.BlockSpec(memory_space=pl.ANY)
    smem_spec = pl.BlockSpec(memory_space=pltpu.SMEM)
    bf16 = jnp.bfloat16
    return pl.pallas_call(
        kernel,
        out_shape=jax.ShapeDtypeStruct(charges.shape, bf16),
        in_specs=[any_spec] * 4 + [smem_spec] * 2,
        out_specs=any_spec,
        scratch_shapes=[
            pltpu.VMEM(charges.shape, bf16),
            pltpu.VMEM(interp_basis.shape, bf16),
            pltpu.VMEM(coupling.shape, bf16),
            pltpu.VMEM(expand_basis.shape, bf16),
            pltpu.VMEM(charges.shape, bf16),
            pltpu.SMEM((2, side, blocks), jnp.int32),
            *[pltpu.VMEM((side, blocks, rows // 2, rank), bf16)] * 2,
            pltpu.VMEM((2, side - 1, blocks, rows // 2, rank), bf16),
            *[pltpu.VMEM((side, blocks, rows // 2, rank), bf16)] * 2,
            pltpu.VMEM((LEVELS + 1, blocks, rows, rank), bf16),
            pltpu.VMEM((LEVELS, blocks, rows, rank), bf16),
            pltpu.SemaphoreType.DMA((4,)),
            *[pltpu.SemaphoreType.DMA((2 * (side - 1),))] * 6,
            pltpu.SemaphoreType.DMA((LEVELS,)),
            pltpu.SemaphoreType.DMA((LEVELS,)),
            pltpu.SemaphoreType.DMA((blocks,)),
        ],
        compiler_params=pltpu.CompilerParams(
            collective_id=0, has_side_effects=True, vmem_limit_bytes=60 * 1024 * 1024
        ),
    )(charges, interp_basis, coupling, expand_basis, block_rank.T, leaf_partner)


def solution(mesh):
    in_specs = (
        P(None, ("grp", "leaf")),
        P(("grp", "leaf"), None, None),
        P(None, ("grp", "leaf"), None, None, None),
        P(("grp", "leaf"), None, None),
        P(None, ("grp", "leaf")),
        P(("grp", "leaf")),
    )
    out_specs = P(None, ("grp", "leaf"))
    return jax.shard_map(shards, mesh=mesh, in_specs=in_specs, out_specs=out_specs, check_vma=False)
```

```python
import math

import jax
import jax.numpy as jnp
from jax import lax
from jax.experimental import pallas as pl
from jax.experimental.pallas import tpu as pltpu
from jax.sharding import PartitionSpec as P

LEVELS = 3
PARTS = 2
MESH = pl.DeviceIdType.MESH


def dot(a, b):
    return jnp.dot(a, b, preferred_element_type=jnp.float32)


def kernel(
    charges_hbm, interp_hbm, coupling_hbm, expand_hbm, rank_ref, partner_ref, out,
    charges, interp, coupling, expand, wanted, picked, state, other,
    load_sems, ask_send, ask_recv, near_send, near_recv, far_send, far_recv,
    level_send, level_recv, answer, *gathered,
):
    near, found = gathered[:PARTS], gathered[PARTS:]
    grp, leaf = lax.axis_index("grp"), lax.axis_index("leaf")
    n_leaf = lax.axis_size("leaf")
    side = near[0].shape[0]
    grp_bits = lax.axis_size("grp").bit_length() - 1
    blocks, size_m, rank = interp.shape
    rows = charges.shape[0]
    part = rows // PARTS

    place = (leaf // side, lax.rem(leaf, side))

    def peer(axis, step):
        at = lax.rem(place[axis] + step, side)
        return at, (at * side + place[1] if axis == 0 else place[0] * side + at)

    pairs, strides = [], []
    for level in range(LEVELS):
        stride = 1 << ((level + 1) * grp_bits // LEVELS - 1)
        strides.append(stride)
        pairs.append(grp + stride * (1 - 2 * lax.rem(grp // stride, 2)))
    barrier = pltpu.get_barrier_semaphore()
    upper = lax.rem(grp // strides[1], 2)

    def greet(pair):
        pl.semaphore_signal(barrier, inc=1, device_id=(pair, leaf), device_id_type=MESH)

    greet(pairs[0])
    greet(pairs[2])
    pl.when(upper == 0)(lambda: greet(pairs[1]))
    for axis in range(2):
        for step in range(1, side):
            pl.semaphore_signal(
                barrier, inc=1, device_id=(grp, peer(axis, step)[1]), device_id_type=MESH
            )

    loads = [
        pltpu.make_async_copy(src, dst, load_sems.at[i])
        for i, (src, dst) in enumerate(
            ((charges_hbm, charges), (interp_hbm, interp), (coupling_hbm, coupling), (expand_hbm, expand))
        )
    ]
    loads[0].start()
    loads[1].start()

    def remote(src, dst, send_sem, recv_sem, device):
        return pltpu.make_async_remote_copy(
            src_ref=src, dst_ref=dst, send_sem=send_sem, recv_sem=recv_sem,
            device_id=device, device_id_type=MESH,
        )

    cols = lax.broadcasted_iota(jnp.int32, (rows, rank), 1)

    def keep(section, block, values):
        mask = cols[: values.shape[0]] < rank_ref[block, section]
        return jnp.where(mask, values, 0.0).astype(jnp.bfloat16)

    loads[0].wait()
    loads[1].wait()
    loads[2].start()
    loads[3].start()
    leaves = []
    for block in range(blocks):
        made = keep(0, block, dot(charges[:, pl.ds(block * size_m, size_m)], interp[block]))
        leaves.append(made)
        for q in range(PARTS):
            near[q][place[q % 2], block] = made[q * part : (q + 1) * part]

    pl.semaphore_wait(barrier, 2 * (side - 1) + LEVELS - 1 + upper)

    @pl.when(upper == 1)
    def _():
        pl.semaphore_signal(answer, inc=1, device_id=(pairs[1], leaf), device_id_type=MESH)

    asks = []
    for axis in range(2):
        for step in range(1, side):
            k = axis * (side - 1) + step - 1
            ask = remote(
                partner_ref, wanted.at[axis, place[axis]], ask_send.at[k], ask_recv.at[k],
                (grp, peer(axis, step)[1]),
            )
            ask.start()
            asks.append(ask)
    nears = [[] for _ in range(PARTS)]
    for q in range(PARTS):
        for step in range(1, side):
            mine = near[q].at[place[q % 2]]
            send = remote(
                mine, mine, near_send.at[q, step - 1], near_recv.at[q, step - 1],
                (grp, peer(q % 2, step)[1]),
            )
            send.start()
            nears[q].append(send)

    loads[2].wait()
    whole = [dot(leaves[block], coupling[0, block, 0]) for block in range(blocks)]
    for ask in asks:
        ask.wait_recv()

    def origin(value):
        at = lax.bitwise_and(value, blocks * n_leaf - 1)
        device, block = lax.shift_right_logical(at, blocks.bit_length() - 1), lax.bitwise_and(at, blocks - 1)
        z_bits = side.bit_length() - 1
        return (lax.shift_right_logical(device, z_bits), lax.bitwise_and(device, side - 1)), block

    sources = [origin(partner_ref[block]) for block in range(blocks)]
    asked = [
        [[origin(wanted[axis, peer(axis, step)[0], block]) for block in range(blocks)] for step in range(1, side)]
        for axis in range(2)
    ]

    fars = [[] for _ in range(PARTS)]
    swaps = [[None] * PARTS for _ in range(LEVELS)]
    owns = [[None] * PARTS for _ in range(LEVELS)]

    def pick(q):
        first, second = q % 2, 1 - q % 2
        for send in nears[q]:
            send.wait_recv()
        for step in range(1, side):
            device = peer(second, step)[1]
            for block in range(blocks):
                source, index = asked[second][step - 1][block]
                picked[q, step - 1, block] = near[q][source[first], index]
            send = remote(
                picked.at[q, step - 1], found[q].at[place[second]],
                far_send.at[q, step - 1], far_recv.at[q, step - 1], (grp, device),
            )
            send.start()
            fars[q].append(send)
        for block in range(blocks):
            source, index = sources[block]
            found[q][place[second], block] = near[q][source[first], index]

    def send_level(level, q):
        swap = remote(
            state.at[level, q], other.at[level, q], level_send.at[level, q], level_recv.at[level, q],
            (pairs[level], leaf),
        )
        swap.start()
        swaps[level][q] = swap

    def own_level(level, q):
        owns[level][q] = [
            dot(state[level, q, block], coupling[level + 1, block, 0]) for block in range(blocks)
        ]

    def leaf_step(q):
        for send in fars[q]:
            send.wait_recv()
        for block in range(blocks):
            source, _ = sources[block]
            total = dot(found[q][source[1 - q % 2], block], coupling[0, block, 1])
            state[0, q, block] = keep(1, block, whole[block][q * part : (q + 1) * part] + total)
        send_level(0, q)
        own_level(0, q)

    def level_step(level, q):
        swaps[level][q].wait_recv()
        for block in range(blocks):
            total = owns[level][q][block] + dot(other[level, q, block], coupling[level + 1, block, 1])
            state[level + 1, q, block] = keep(level + 2, block, total)
        if level + 1 < LEVELS:
            send_level(level + 1, q)
            own_level(level + 1, q)

    def expand_step(q):
        here = pl.ds(q * part, part)
        for block in range(blocks):
            out[here, pl.ds(block * size_m, size_m)] = dot(state[LEVELS, q, block], expand[block]).astype(
                jnp.bfloat16
            )

    for q in range(PARTS):
        pick(q)
    for q in range(PARTS + 1):
        if q < PARTS:
            leaf_step(q)
        if q == 1:
            pl.when(upper == 0)(lambda: pl.semaphore_wait(answer, 1))
        if q >= 1:
            level_step(0, q - 1)
    loads[3].wait()
    for send in asks + sum(nears + fars, []) + swaps[0]:
        send.wait_send()
    lag = PARTS // 2
    for q in range(PARTS + lag):
        if q < PARTS:
            level_step(1, q)
        if q >= lag:
            level_step(2, q - lag)
            expand_step(q - lag)
    for send in swaps[1] + swaps[2]:
        send.wait_send()


def shards(charges, interp_basis, coupling, expand_basis, block_rank, leaf_partner):
    side = math.isqrt(lax.axis_size("leaf"))
    blocks, size_m, rank = interp_basis.shape
    rows = charges.shape[0]
    part = rows // PARTS
    any_spec = pl.BlockSpec(memory_space=pltpu.HBM)
    smem_spec = pl.BlockSpec(memory_space=pltpu.SMEM)
    bf16 = jnp.bfloat16
    dma = pltpu.SemaphoreType.DMA
    return pl.pallas_call(
        kernel,
        out_shape=pltpu.VMEM(charges.shape, bf16),
        in_specs=[any_spec] * 4 + [smem_spec] * 2,
        out_specs=pl.BlockSpec(memory_space=pltpu.VMEM),
        scratch_shapes=[
            pltpu.VMEM(charges.shape, bf16),
            pltpu.VMEM(interp_basis.shape, bf16),
            pltpu.VMEM(coupling.shape, bf16),
            pltpu.VMEM(expand_basis.shape, bf16),
            pltpu.SMEM((2, side, blocks), jnp.int32),
            pltpu.VMEM((PARTS, side - 1, blocks, part, rank), bf16),
            pltpu.VMEM((LEVELS + 1, PARTS, blocks, part, rank), bf16),
            pltpu.VMEM((LEVELS, PARTS, blocks, part, rank), bf16),
            dma((4,)),
            *[dma((2 * (side - 1),))] * 2,
            *[dma((PARTS, side - 1))] * 4,
            *[dma((LEVELS, PARTS))] * 2,
            pltpu.SemaphoreType.REGULAR,
            *[pltpu.VMEM((side, blocks, part, rank), bf16)] * (2 * PARTS),
        ],
        compiler_params=pltpu.CompilerParams(
            collective_id=0, has_side_effects=True, vmem_limit_bytes=60 * 1024 * 1024
        ),
    )(charges, interp_basis, coupling, expand_basis, block_rank.T, leaf_partner)


def solution(mesh):
    in_specs = (
        P(None, ("grp", "leaf")),
        P(("grp", "leaf"), None, None),
        P(None, ("grp", "leaf"), None, None, None),
        P(("grp", "leaf"), None, None),
        P(None, ("grp", "leaf")),
        P(("grp", "leaf")),
    )
    out_specs = P(None, ("grp", "leaf"))
    return jax.shard_map(shards, mesh=mesh, in_specs=in_specs, out_specs=out_specs, check_vma=False)
```

```python
import math

import jax
import jax.numpy as jnp
from jax import lax
from jax.experimental import pallas as pl
from jax.experimental.pallas import tpu as pltpu
from jax.sharding import PartitionSpec as P

LEVELS = 3
PARTS = 2
MESH = pl.DeviceIdType.MESH


def dot(a, b):
    return jnp.dot(a, b, preferred_element_type=jnp.float32)


def kernel(
    charges_hbm, interp_hbm, coupling_hbm, expand_hbm, rank_hbm, partner_hbm, out,
    charges, interp, coupling, expand, rank_ref, partner_ref, wanted, picked, state, other,
    load_sems, ask_send, ask_recv, near_send, near_recv, far_send, far_recv,
    level_send, level_recv, answer, *gathered,
):
    near, found = gathered[:PARTS], gathered[PARTS:]
    grp, leaf = lax.axis_index("grp"), lax.axis_index("leaf")
    n_leaf = lax.axis_size("leaf")
    side = near[0].shape[0]
    grp_bits = lax.axis_size("grp").bit_length() - 1
    blocks, size_m, rank = interp.shape
    rows = charges.shape[0]
    part = rows // PARTS

    place = (leaf // side, lax.rem(leaf, side))

    def peer(axis, step):
        at = lax.rem(place[axis] + step, side)
        return at, (at * side + place[1] if axis == 0 else place[0] * side + at)

    pairs, strides = [], []
    for level in range(LEVELS):
        stride = 1 << ((level + 1) * grp_bits // LEVELS - 1)
        strides.append(stride)
        pairs.append(grp + stride * (1 - 2 * lax.rem(grp // stride, 2)))
    barrier = pltpu.get_barrier_semaphore()
    upper = lax.rem(grp // strides[1], 2)

    def greet(pair):
        pl.semaphore_signal(barrier, inc=1, device_id=(pair, leaf), device_id_type=MESH)

    greet(pairs[0])
    greet(pairs[2])
    pl.when(upper == 0)(lambda: greet(pairs[1]))
    for axis in range(2):
        for step in range(1, side):
            pl.semaphore_signal(
                barrier, inc=1, device_id=(grp, peer(axis, step)[1]), device_id_type=MESH
            )

    loads = [
        pltpu.make_async_copy(src, dst, load_sems.at[i])
        for i, (src, dst) in enumerate(
            (
                (charges_hbm, charges), (interp_hbm, interp), (coupling_hbm, coupling), (expand_hbm, expand),
                (rank_hbm, rank_ref), (partner_hbm, partner_ref),
            )
        )
    ]
    for i in (4, 5, 0, 1):
        loads[i].start()

    def remote(src, dst, send_sem, recv_sem, device):
        return pltpu.make_async_remote_copy(
            src_ref=src, dst_ref=dst, send_sem=send_sem, recv_sem=recv_sem,
            device_id=device, device_id_type=MESH,
        )

    cols = lax.broadcasted_iota(jnp.int32, (rows, rank), 1)

    def keep(section, block, values):
        mask = cols[: values.shape[0]] < rank_ref[block, section]
        return jnp.where(mask, values, 0.0).astype(jnp.bfloat16)

    for i in (4, 5, 0, 1):
        loads[i].wait()
    loads[2].start()
    loads[3].start()
    leaves = []
    for block in range(blocks):
        made = keep(0, block, dot(charges[:, pl.ds(block * size_m, size_m)], interp[block]))
        leaves.append(made)
        for q in range(PARTS):
            near[q][place[q % 2], block] = made[q * part : (q + 1) * part]

    pl.semaphore_wait(barrier, 2 * (side - 1) + LEVELS - 1 + upper)

    @pl.when(upper == 1)
    def _():
        pl.semaphore_signal(answer, inc=1, device_id=(pairs[1], leaf), device_id_type=MESH)

    asks = []
    for axis in range(2):
        for step in range(1, side):
            k = axis * (side - 1) + step - 1
            ask = remote(
                partner_ref, wanted.at[axis, place[axis]], ask_send.at[k], ask_recv.at[k],
                (grp, peer(axis, step)[1]),
            )
            ask.start()
            asks.append(ask)
    nears = [[] for _ in range(PARTS)]
    for q in range(PARTS):
        for step in range(1, side):
            mine = near[q].at[place[q % 2]]
            send = remote(
                mine, mine, near_send.at[q, step - 1], near_recv.at[q, step - 1],
                (grp, peer(q % 2, step)[1]),
            )
            send.start()
            nears[q].append(send)

    loads[2].wait()
    whole = [dot(leaves[block], coupling[0, block, 0]) for block in range(blocks)]
    for ask in asks:
        ask.wait_recv()

    def origin(value):
        at = lax.bitwise_and(value, blocks * n_leaf - 1)
        device, block = lax.shift_right_logical(at, blocks.bit_length() - 1), lax.bitwise_and(at, blocks - 1)
        z_bits = side.bit_length() - 1
        return (lax.shift_right_logical(device, z_bits), lax.bitwise_and(device, side - 1)), block

    sources = [origin(partner_ref[block]) for block in range(blocks)]
    asked = [
        [[origin(wanted[axis, peer(axis, step)[0], block]) for block in range(blocks)] for step in range(1, side)]
        for axis in range(2)
    ]

    fars = [[] for _ in range(PARTS)]
    swaps = [[None] * PARTS for _ in range(LEVELS)]
    owns = [[None] * PARTS for _ in range(LEVELS)]

    def pick(q):
        first, second = q % 2, 1 - q % 2
        for send in nears[q]:
            send.wait_recv()
        for step in range(1, side):
            device = peer(second, step)[1]
            for block in range(blocks):
                source, index = asked[second][step - 1][block]
                picked[q, step - 1, block] = near[q][source[first], index]
            send = remote(
                picked.at[q, step - 1], found[q].at[place[second]],
                far_send.at[q, step - 1], far_recv.at[q, step - 1], (grp, device),
            )
            send.start()
            fars[q].append(send)
        for block in range(blocks):
            source, index = sources[block]
            found[q][place[second], block] = near[q][source[first], index]

    def send_level(level, q):
        swap = remote(
            state.at[level, q], other.at[level, q], level_send.at[level, q], level_recv.at[level, q],
            (pairs[level], leaf),
        )
        swap.start()
        swaps[level][q] = swap

    def own_level(level, q):
        owns[level][q] = [
            dot(state[level, q, block], coupling[level + 1, block, 0]) for block in range(blocks)
        ]

    def leaf_step(q):
        for send in fars[q]:
            send.wait_recv()
        for block in range(blocks):
            source, _ = sources[block]
            total = dot(found[q][source[1 - q % 2], block], coupling[0, block, 1])
            state[0, q, block] = keep(1, block, whole[block][q * part : (q + 1) * part] + total)
        send_level(0, q)
        own_level(0, q)

    def level_step(level, q):
        swaps[level][q].wait_recv()
        for block in range(blocks):
            total = owns[level][q][block] + dot(other[level, q, block], coupling[level + 1, block, 1])
            state[level + 1, q, block] = keep(level + 2, block, total)
        if level + 1 < LEVELS:
            send_level(level + 1, q)
            own_level(level + 1, q)

    def expand_step(q):
        here = pl.ds(q * part, part)
        for block in range(blocks):
            out[here, pl.ds(block * size_m, size_m)] = dot(state[LEVELS, q, block], expand[block]).astype(
                jnp.bfloat16
            )

    for q in range(PARTS):
        pick(q)
    for q in range(PARTS + 1):
        if q < PARTS:
            leaf_step(q)
        if q == 1:
            pl.when(upper == 0)(lambda: pl.semaphore_wait(answer, 1))
        if q >= 1:
            level_step(0, q - 1)
    loads[3].wait()
    for send in asks + sum(nears + fars, []) + swaps[0]:
        send.wait_send()
    lag = PARTS // 2
    for q in range(PARTS + lag):
        if q < PARTS:
            level_step(1, q)
        if q >= lag:
            level_step(2, q - lag)
            expand_step(q - lag)
    for send in swaps[1] + swaps[2]:
        send.wait_send()


def shards(charges, interp_basis, coupling, expand_basis, block_rank, leaf_partner):
    side = math.isqrt(lax.axis_size("leaf"))
    blocks, size_m, rank = interp_basis.shape
    rows = charges.shape[0]
    part = rows // PARTS
    hbm_spec = pl.BlockSpec(memory_space=pltpu.HBM)
    bf16 = jnp.bfloat16
    dma = pltpu.SemaphoreType.DMA
    return pl.pallas_call(
        kernel,
        out_shape=pltpu.VMEM(charges.shape, bf16),
        in_specs=[hbm_spec] * 6,
        out_specs=pl.BlockSpec(memory_space=pltpu.VMEM),
        scratch_shapes=[
            pltpu.VMEM(charges.shape, bf16),
            pltpu.VMEM(interp_basis.shape, bf16),
            pltpu.VMEM(coupling.shape, bf16),
            pltpu.VMEM(expand_basis.shape, bf16),
            pltpu.SMEM(block_rank.shape[::-1], jnp.int32),
            pltpu.SMEM(leaf_partner.shape, jnp.int32),
            pltpu.SMEM((2, side, blocks), jnp.int32),
            pltpu.VMEM((PARTS, side - 1, blocks, part, rank), bf16),
            pltpu.VMEM((LEVELS + 1, PARTS, blocks, part, rank), bf16),
            pltpu.VMEM((LEVELS, PARTS, blocks, part, rank), bf16),
            dma((6,)),
            *[dma((2 * (side - 1),))] * 2,
            *[dma((PARTS, side - 1))] * 4,
            *[dma((LEVELS, PARTS))] * 2,
            pltpu.SemaphoreType.REGULAR,
            *[pltpu.VMEM((side, blocks, part, rank), bf16)] * (2 * PARTS),
        ],
        compiler_params=pltpu.CompilerParams(
            collective_id=0, has_side_effects=True, vmem_limit_bytes=60 * 1024 * 1024
        ),
    )(charges, interp_basis, coupling, expand_basis, block_rank.T, leaf_partner)


def solution(mesh):
    in_specs = (
        P(None, ("grp", "leaf")),
        P(("grp", "leaf"), None, None),
        P(None, ("grp", "leaf"), None, None, None),
        P(("grp", "leaf"), None, None),
        P(None, ("grp", "leaf")),
        P(("grp", "leaf")),
    )
    out_specs = P(None, ("grp", "leaf"))
    return jax.shard_map(shards, mesh=mesh, in_specs=in_specs, out_specs=out_specs, check_vma=False)
```

```python
import math

import jax
import jax.numpy as jnp
from jax import lax
from jax.experimental import pallas as pl
from jax.experimental.pallas import tpu as pltpu
from jax.sharding import PartitionSpec as P

LEVELS = 3
PARTS = 2
MESH = pl.DeviceIdType.MESH


def dot(a, b):
    return jnp.dot(a, b, preferred_element_type=jnp.float32)


def kernel(
    charges_hbm, interp_hbm, coupling_hbm, expand_hbm, rank_hbm, partner_hbm, out,
    charges, interp, coupling, expand, rank_ref, partner_ref, wanted, picked, state, other,
    load_sems, ask_send, ask_recv, near_send, near_recv, far_send, far_recv,
    level_send, level_recv, answer, *gathered,
):
    near, found = gathered[:PARTS], gathered[PARTS:]
    grp, leaf = lax.axis_index("grp"), lax.axis_index("leaf")
    n_leaf = lax.axis_size("leaf")
    side = near[0].shape[0]
    grp_bits = lax.axis_size("grp").bit_length() - 1
    blocks, size_m, rank = interp.shape
    rows = charges.shape[0]
    part = rows // PARTS

    place = (leaf // side, lax.rem(leaf, side))

    def peer(axis, step):
        at = lax.rem(place[axis] + step, side)
        return at, (at * side + place[1] if axis == 0 else place[0] * side + at)

    pairs, strides = [], []
    for level in range(LEVELS):
        stride = 1 << ((level + 1) * grp_bits // LEVELS - 1)
        strides.append(stride)
        pairs.append(grp + stride * (1 - 2 * lax.rem(grp // stride, 2)))
    barrier = pltpu.get_barrier_semaphore()
    upper = lax.rem(grp // strides[1], 2)

    def greet(pair):
        pl.semaphore_signal(barrier, inc=1, device_id=(pair, leaf), device_id_type=MESH)

    greet(pairs[0])
    greet(pairs[2])
    pl.when(upper == 0)(lambda: greet(pairs[1]))
    for axis in range(2):
        for step in range(1, side):
            pl.semaphore_signal(
                barrier, inc=1, device_id=(grp, peer(axis, step)[1]), device_id_type=MESH
            )

    loads = [
        pltpu.make_async_copy(src, dst, load_sems.at[i])
        for i, (src, dst) in enumerate(
            (
                (charges_hbm, charges), (interp_hbm, interp), (coupling_hbm, coupling), (expand_hbm, expand),
                (rank_hbm, rank_ref), (partner_hbm, partner_ref),
            )
        )
    ]
    for i in (4, 5, 0, 1):
        loads[i].start()

    def remote(src, dst, send_sem, recv_sem, device):
        return pltpu.make_async_remote_copy(
            src_ref=src, dst_ref=dst, send_sem=send_sem, recv_sem=recv_sem,
            device_id=device, device_id_type=MESH,
        )

    cols = lax.broadcasted_iota(jnp.int32, (rows, rank), 1)

    def keep(section, block, values):
        mask = cols[: values.shape[0]] < rank_ref[block, section]
        return jnp.where(mask, values, 0.0).astype(jnp.bfloat16)

    for i in (4, 5, 0, 1):
        loads[i].wait()
    loads[2].start()
    loads[3].start()
    leaves = []
    for block in range(blocks):
        made = keep(0, block, dot(charges[:, pl.ds(block * size_m, size_m)], interp[block]))
        leaves.append(made)
        for q in range(PARTS):
            near[q][place[q % 2], block] = made[q * part : (q + 1) * part]

    pl.semaphore_wait(barrier, 2 * (side - 1) + LEVELS - 1 + upper)

    @pl.when(upper == 1)
    def _():
        pl.semaphore_signal(answer, inc=1, device_id=(pairs[1], leaf), device_id_type=MESH)

    asks = []
    for axis in range(2):
        for step in range(1, side):
            k = axis * (side - 1) + step - 1
            ask = remote(
                partner_ref, wanted.at[axis, place[axis]], ask_send.at[k], ask_recv.at[k],
                (grp, peer(axis, step)[1]),
            )
            ask.start()
            asks.append(ask)
    nears = [[] for _ in range(PARTS)]
    for q in range(PARTS):
        for step in range(1, side):
            mine = near[q].at[place[q % 2]]
            send = remote(
                mine, mine, near_send.at[q, step - 1], near_recv.at[q, step - 1],
                (grp, peer(q % 2, step)[1]),
            )
            send.start()
            nears[q].append(send)

    loads[2].wait()
    whole = [dot(leaves[block], coupling[0, block, 0]) for block in range(blocks)]
    for ask in asks:
        ask.wait_recv()

    def origin(value):
        at = lax.bitwise_and(value, blocks * n_leaf - 1)
        device, block = lax.shift_right_logical(at, blocks.bit_length() - 1), lax.bitwise_and(at, blocks - 1)
        z_bits = side.bit_length() - 1
        return (lax.shift_right_logical(device, z_bits), lax.bitwise_and(device, side - 1)), block

    sources = [origin(partner_ref[block]) for block in range(blocks)]
    asked = [
        [[origin(wanted[axis, peer(axis, step)[0], block]) for block in range(blocks)] for step in range(1, side)]
        for axis in range(2)
    ]

    fars = [[] for _ in range(PARTS)]
    swaps = [[None] * PARTS for _ in range(LEVELS)]
    owns = [[None] * PARTS for _ in range(LEVELS)]

    def pick(q):
        first, second = q % 2, 1 - q % 2
        for send in nears[q]:
            send.wait_recv()
        for step in range(1, side):
            device = peer(second, step)[1]
            for block in range(blocks):
                source, index = asked[second][step - 1][block]
                picked[q, step - 1, block] = near[q][source[first], index]
            send = remote(
                picked.at[q, step - 1], found[q].at[place[second]],
                far_send.at[q, step - 1], far_recv.at[q, step - 1], (grp, device),
            )
            send.start()
            fars[q].append(send)

    def send_level(level, q):
        swap = remote(
            state.at[level, q], other.at[level, q], level_send.at[level, q], level_recv.at[level, q],
            (pairs[level], leaf),
        )
        swap.start()
        swaps[level][q] = swap

    def own_level(level, q):
        owns[level][q] = [
            dot(state[level, q, block], coupling[level + 1, block, 0]) for block in range(blocks)
        ]

    def leaf_step(q):
        for send in fars[q]:
            send.wait_recv()
        for block in range(blocks):
            source, _ = sources[block]
            total = dot(found[q][source[1 - q % 2], block], coupling[0, block, 1])
            state[0, q, block] = keep(1, block, whole[block][q * part : (q + 1) * part] + total)
        send_level(0, q)

    def level_step(level, q):
        swaps[level][q].wait_recv()
        for block in range(blocks):
            total = owns[level][q][block] + dot(other[level, q, block], coupling[level + 1, block, 1])
            state[level + 1, q, block] = keep(level + 2, block, total)
        if level + 1 < LEVELS:
            send_level(level + 1, q)

    def expand_step(q):
        here = pl.ds(q * part, part)
        for block in range(blocks):
            out[here, pl.ds(block * size_m, size_m)] = dot(state[LEVELS, q, block], expand[block]).astype(
                jnp.bfloat16
            )

    for q in range(PARTS):
        pick(q)
    for q in range(PARTS):
        for block in range(blocks):
            source, index = sources[block]
            found[q][place[1 - q % 2], block] = near[q][source[q % 2], index]
    for q in range(PARTS):
        leaf_step(q)
    for q in range(PARTS):
        own_level(0, q)
    pl.when(upper == 0)(lambda: pl.semaphore_wait(answer, 1))
    for q in range(PARTS):
        level_step(0, q)
    for q in range(PARTS):
        own_level(1, q)
    loads[3].wait()
    for send in asks + sum(nears + fars, []) + swaps[0]:
        send.wait_send()
    for q in range(PARTS):
        level_step(1, q)
    for q in range(PARTS):
        own_level(2, q)
    for q in range(PARTS):
        level_step(2, q)
        expand_step(q)
    for send in swaps[1] + swaps[2]:
        send.wait_send()


def shards(charges, interp_basis, coupling, expand_basis, block_rank, leaf_partner):
    side = math.isqrt(lax.axis_size("leaf"))
    blocks, size_m, rank = interp_basis.shape
    rows = charges.shape[0]
    part = rows // PARTS
    hbm_spec = pl.BlockSpec(memory_space=pltpu.HBM)
    bf16 = jnp.bfloat16
    dma = pltpu.SemaphoreType.DMA
    return pl.pallas_call(
        kernel,
        out_shape=pltpu.VMEM(charges.shape, bf16),
        in_specs=[hbm_spec] * 6,
        out_specs=pl.BlockSpec(memory_space=pltpu.VMEM),
        scratch_shapes=[
            pltpu.VMEM(charges.shape, bf16),
            pltpu.VMEM(interp_basis.shape, bf16),
            pltpu.VMEM(coupling.shape, bf16),
            pltpu.VMEM(expand_basis.shape, bf16),
            pltpu.SMEM(block_rank.shape[::-1], jnp.int32),
            pltpu.SMEM(leaf_partner.shape, jnp.int32),
            pltpu.SMEM((2, side, blocks), jnp.int32),
            pltpu.VMEM((PARTS, side - 1, blocks, part, rank), bf16),
            pltpu.VMEM((LEVELS + 1, PARTS, blocks, part, rank), bf16),
            pltpu.VMEM((LEVELS, PARTS, blocks, part, rank), bf16),
            dma((6,)),
            *[dma((2 * (side - 1),))] * 2,
            *[dma((PARTS, side - 1))] * 4,
            *[dma((LEVELS, PARTS))] * 2,
            pltpu.SemaphoreType.REGULAR,
            *[pltpu.VMEM((side, blocks, part, rank), bf16)] * (2 * PARTS),
        ],
        compiler_params=pltpu.CompilerParams(
            collective_id=0, has_side_effects=True, vmem_limit_bytes=60 * 1024 * 1024
        ),
    )(charges, interp_basis, coupling, expand_basis, block_rank.T, leaf_partner)


def solution(mesh):
    in_specs = (
        P(None, ("grp", "leaf")),
        P(("grp", "leaf"), None, None),
        P(None, ("grp", "leaf"), None, None, None),
        P(("grp", "leaf"), None, None),
        P(None, ("grp", "leaf")),
        P(("grp", "leaf")),
    )
    out_specs = P(None, ("grp", "leaf"))
    return jax.shard_map(shards, mesh=mesh, in_specs=in_specs, out_specs=out_specs, check_vma=False)
```

```python
import math

import jax
import jax.numpy as jnp
from jax import lax
from jax.experimental import pallas as pl
from jax.experimental.pallas import tpu as pltpu
from jax.sharding import PartitionSpec as P

LEVELS = 3
PARTS = 2
MESH = pl.DeviceIdType.MESH


def dot(a, b):
    return jnp.dot(a, b, preferred_element_type=jnp.float32)


def kernel(
    charges_hbm, interp_hbm, coupling_hbm, expand_hbm, rank_hbm, partner_hbm, out,
    charges, interp, coupling, expand, rank_ref, partner_ref, wanted, picked, state, other,
    load_sems, ask_send, ask_recv, near_send, near_recv, far_send, far_recv,
    level_send, level_recv, answer, *gathered,
):
    near, found = gathered[:PARTS], gathered[PARTS:]
    grp, leaf = lax.axis_index("grp"), lax.axis_index("leaf")
    n_leaf = lax.axis_size("leaf")
    side = near[0].shape[0]
    grp_bits = lax.axis_size("grp").bit_length() - 1
    blocks, size_m, rank = interp.shape
    rows = charges.shape[0]
    part = rows // PARTS

    place = (leaf // side, lax.rem(leaf, side))

    def peer(axis, step):
        at = lax.rem(place[axis] + step, side)
        return at, (at * side + place[1] if axis == 0 else place[0] * side + at)

    pairs, strides = [], []
    for level in range(LEVELS):
        stride = 1 << ((level + 1) * grp_bits // LEVELS - 1)
        strides.append(stride)
        pairs.append(grp + stride * (1 - 2 * lax.rem(grp // stride, 2)))
    barrier = pltpu.get_barrier_semaphore()
    upper = lax.rem(grp // strides[1], 2)

    def greet(pair):
        pl.semaphore_signal(barrier, inc=1, device_id=(pair, leaf), device_id_type=MESH)

    greet(pairs[0])
    greet(pairs[2])
    pl.when(upper == 0)(lambda: greet(pairs[1]))
    for axis in range(2):
        for step in range(1, side):
            pl.semaphore_signal(
                barrier, inc=1, device_id=(grp, peer(axis, step)[1]), device_id_type=MESH
            )

    loads = [
        pltpu.make_async_copy(src, dst, load_sems.at[i])
        for i, (src, dst) in enumerate(
            (
                (charges_hbm, charges), (interp_hbm, interp), (coupling_hbm, coupling), (expand_hbm, expand),
                (rank_hbm, rank_ref), (partner_hbm, partner_ref),
            )
        )
    ]
    for i in (4, 5, 0, 1):
        loads[i].start()

    def remote(src, dst, send_sem, recv_sem, device):
        return pltpu.make_async_remote_copy(
            src_ref=src, dst_ref=dst, send_sem=send_sem, recv_sem=recv_sem,
            device_id=device, device_id_type=MESH,
        )

    cols = lax.broadcasted_iota(jnp.int32, (rows, rank), 1)

    def keep(section, block, values):
        mask = cols[: values.shape[0]] < rank_ref[block, section]
        return jnp.where(mask, values, 0.0).astype(jnp.bfloat16)

    for i in (4, 5, 0, 1):
        loads[i].wait()
    loads[2].start()
    loads[3].start()
    leaves = []
    for block in range(blocks):
        made = keep(0, block, dot(charges[:, pl.ds(block * size_m, size_m)], interp[block]))
        leaves.append(made)
        for q in range(PARTS):
            near[q][place[q % 2], block] = made[q * part : (q + 1) * part]

    pl.semaphore_wait(barrier, 2 * (side - 1) + LEVELS - 1 + upper)

    asks = []
    for axis in range(2):
        for step in range(1, side):
            k = axis * (side - 1) + step - 1
            ask = remote(
                partner_ref, wanted.at[axis, place[axis]], ask_send.at[k], ask_recv.at[k],
                (grp, peer(axis, step)[1]),
            )
            ask.start()
            asks.append(ask)
    nears = [[] for _ in range(PARTS)]
    for q in range(PARTS):
        for step in range(1, side):
            mine = near[q].at[place[q % 2]]
            send = remote(
                mine, mine, near_send.at[q, step - 1], near_recv.at[q, step - 1],
                (grp, peer(q % 2, step)[1]),
            )
            send.start()
            nears[q].append(send)

    loads[2].wait()
    whole = [dot(leaves[block], coupling[0, block, 0]) for block in range(blocks)]
    for ask in asks:
        ask.wait_recv()

    def origin(value):
        at = lax.bitwise_and(value, blocks * n_leaf - 1)
        device, block = lax.shift_right_logical(at, blocks.bit_length() - 1), lax.bitwise_and(at, blocks - 1)
        z_bits = side.bit_length() - 1
        return (lax.shift_right_logical(device, z_bits), lax.bitwise_and(device, side - 1)), block

    sources = [origin(partner_ref[block]) for block in range(blocks)]
    asked = [
        [[origin(wanted[axis, peer(axis, step)[0], block]) for block in range(blocks)] for step in range(1, side)]
        for axis in range(2)
    ]

    fars = [[] for _ in range(PARTS)]
    swaps = [[None] * PARTS for _ in range(LEVELS)]
    owns = [[None] * PARTS for _ in range(LEVELS)]

    def pick(q):
        first, second = q % 2, 1 - q % 2
        for send in nears[q]:
            send.wait_recv()
        for step in range(1, side):
            device = peer(second, step)[1]
            for block in range(blocks):
                source, index = asked[second][step - 1][block]
                picked[q, step - 1, block] = near[q][source[first], index]
            send = remote(
                picked.at[q, step - 1], found[q].at[place[second]],
                far_send.at[q, step - 1], far_recv.at[q, step - 1], (grp, device),
            )
            send.start()
            fars[q].append(send)

    def send_level(level, q):
        swap = remote(
            state.at[level, q], other.at[level, q], level_send.at[level, q], level_recv.at[level, q],
            (pairs[level], leaf),
        )
        swap.start()
        swaps[level][q] = swap

    def own_level(level, q):
        owns[level][q] = [
            dot(state[level, q, block], coupling[level + 1, block, 0]) for block in range(blocks)
        ]

    def leaf_step(q):
        for send in fars[q]:
            send.wait_recv()
        for block in range(blocks):
            source, _ = sources[block]
            total = dot(found[q][source[1 - q % 2], block], coupling[0, block, 1])
            state[0, q, block] = keep(1, block, whole[block][q * part : (q + 1) * part] + total)
        send_level(0, q)

    def level_step(level, q):
        swaps[level][q].wait_recv()
        for block in range(blocks):
            total = owns[level][q][block] + dot(other[level, q, block], coupling[level + 1, block, 1])
            state[level + 1, q, block] = keep(level + 2, block, total)
        if level + 1 < LEVELS:
            send_level(level + 1, q)

    def expand_step(q):
        here = pl.ds(q * part, part)
        for block in range(blocks):
            out[here, pl.ds(block * size_m, size_m)] = dot(state[LEVELS, q, block], expand[block]).astype(
                jnp.bfloat16
            )

    for q in range(PARTS):
        pick(q)
    @pl.when(jnp.logical_and(upper == 1, lax.rem(place[1], 2) == 1))
    def _():
        pl.semaphore_signal(answer, inc=1, device_id=(pairs[1], leaf), device_id_type=MESH)

    for q in range(PARTS):
        for block in range(blocks):
            source, index = sources[block]
            found[q][place[1 - q % 2], block] = near[q][source[q % 2], index]
    for q in range(PARTS):
        leaf_step(q)
    @pl.when(jnp.logical_and(upper == 1, lax.rem(place[1], 2) == 0))
    def _():
        pl.semaphore_signal(answer, inc=1, device_id=(pairs[1], leaf), device_id_type=MESH)

    for q in range(PARTS):
        own_level(0, q)
    pl.when(upper == 0)(lambda: pl.semaphore_wait(answer, 1))
    for q in range(PARTS):
        level_step(0, q)
    for q in range(PARTS):
        own_level(1, q)
    loads[3].wait()
    for send in asks + sum(nears + fars, []) + swaps[0]:
        send.wait_send()
    for q in range(PARTS):
        level_step(1, q)
    for q in range(PARTS):
        own_level(2, q)
    for q in range(PARTS):
        level_step(2, q)
        expand_step(q)
    for send in swaps[1] + swaps[2]:
        send.wait_send()


def shards(charges, interp_basis, coupling, expand_basis, block_rank, leaf_partner):
    side = math.isqrt(lax.axis_size("leaf"))
    blocks, size_m, rank = interp_basis.shape
    rows = charges.shape[0]
    part = rows // PARTS
    hbm_spec = pl.BlockSpec(memory_space=pltpu.HBM)
    bf16 = jnp.bfloat16
    dma = pltpu.SemaphoreType.DMA
    return pl.pallas_call(
        kernel,
        out_shape=pltpu.VMEM(charges.shape, bf16),
        in_specs=[hbm_spec] * 6,
        out_specs=pl.BlockSpec(memory_space=pltpu.VMEM),
        scratch_shapes=[
            pltpu.VMEM(charges.shape, bf16),
            pltpu.VMEM(interp_basis.shape, bf16),
            pltpu.VMEM(coupling.shape, bf16),
            pltpu.VMEM(expand_basis.shape, bf16),
            pltpu.SMEM(block_rank.shape[::-1], jnp.int32),
            pltpu.SMEM(leaf_partner.shape, jnp.int32),
            pltpu.SMEM((2, side, blocks), jnp.int32),
            pltpu.VMEM((PARTS, side - 1, blocks, part, rank), bf16),
            pltpu.VMEM((LEVELS + 1, PARTS, blocks, part, rank), bf16),
            pltpu.VMEM((LEVELS, PARTS, blocks, part, rank), bf16),
            dma((6,)),
            *[dma((2 * (side - 1),))] * 2,
            *[dma((PARTS, side - 1))] * 4,
            *[dma((LEVELS, PARTS))] * 2,
            pltpu.SemaphoreType.REGULAR,
            *[pltpu.VMEM((side, blocks, part, rank), bf16)] * (2 * PARTS),
        ],
        compiler_params=pltpu.CompilerParams(
            collective_id=0, has_side_effects=True, vmem_limit_bytes=60 * 1024 * 1024
        ),
    )(charges, interp_basis, coupling, expand_basis, block_rank.T, leaf_partner)


def solution(mesh):
    in_specs = (
        P(None, ("grp", "leaf")),
        P(("grp", "leaf"), None, None),
        P(None, ("grp", "leaf"), None, None, None),
        P(("grp", "leaf"), None, None),
        P(None, ("grp", "leaf")),
        P(("grp", "leaf")),
    )
    out_specs = P(None, ("grp", "leaf"))
    return jax.shard_map(shards, mesh=mesh, in_specs=in_specs, out_specs=out_specs, check_vma=False)
```

```python
import math

import jax
import jax.numpy as jnp
from jax import lax
from jax.experimental import pallas as pl
from jax.experimental.pallas import tpu as pltpu
from jax.sharding import PartitionSpec as P

LEVELS = 3
PARTS = 2
MESH = pl.DeviceIdType.MESH


def dot(a, b):
    return jnp.dot(a, b, preferred_element_type=jnp.float32)


def kernel(
    charges_hbm, interp_hbm, coupling_hbm, expand_hbm, rank_hbm, partner_hbm, out,
    charges, interp, coupling, expand, rank_ref, partner_ref, wanted, picked, state, other,
    load_sems, ask_send, ask_recv, near_send, near_recv, far_send, far_recv,
    level_send, level_recv, answer, folded, *gathered,
):
    near, found = gathered[:PARTS], gathered[PARTS:]
    grp, leaf = lax.axis_index("grp"), lax.axis_index("leaf")
    n_leaf = lax.axis_size("leaf")
    side = near[0].shape[0]
    grp_bits = lax.axis_size("grp").bit_length() - 1
    blocks, size_m, rank = interp.shape
    rows = charges.shape[0]
    part = rows // PARTS

    place = (leaf // side, lax.rem(leaf, side))

    def peer(axis, step):
        at = lax.rem(place[axis] + step, side)
        return at, (at * side + place[1] if axis == 0 else place[0] * side + at)

    pairs, strides = [], []
    for level in range(LEVELS):
        stride = 1 << ((level + 1) * grp_bits // LEVELS - 1)
        strides.append(stride)
        pairs.append(grp + stride * (1 - 2 * lax.rem(grp // stride, 2)))
    barrier = pltpu.get_barrier_semaphore()
    upper = lax.rem(grp // strides[1], 2)

    def greet(pair):
        pl.semaphore_signal(barrier, inc=1, device_id=(pair, leaf), device_id_type=MESH)

    greet(pairs[0])
    greet(pairs[2])
    pl.when(upper == 0)(lambda: greet(pairs[1]))
    for axis in range(2):
        for step in range(1, side):
            pl.semaphore_signal(
                barrier, inc=1, device_id=(grp, peer(axis, step)[1]), device_id_type=MESH
            )

    loads = [
        pltpu.make_async_copy(src, dst, load_sems.at[i])
        for i, (src, dst) in enumerate(
            (
                (charges_hbm, charges), (interp_hbm, interp), (coupling_hbm, coupling), (expand_hbm, expand),
                (rank_hbm, rank_ref), (partner_hbm, partner_ref),
            )
        )
    ]
    for i in (4, 5, 0, 1):
        loads[i].start()

    def remote(src, dst, send_sem, recv_sem, device):
        return pltpu.make_async_remote_copy(
            src_ref=src, dst_ref=dst, send_sem=send_sem, recv_sem=recv_sem,
            device_id=device, device_id_type=MESH,
        )

    cols = lax.broadcasted_iota(jnp.int32, (rows, rank), 1)

    def keep(section, block, values):
        mask = cols[: values.shape[0]] < rank_ref[block, section]
        return jnp.where(mask, values, 0.0).astype(jnp.bfloat16)

    for i in (4, 5, 0, 1):
        loads[i].wait()
    loads[2].start()
    loads[3].start()
    leaves = []
    for block in range(blocks):
        made = keep(0, block, dot(charges[:, pl.ds(block * size_m, size_m)], interp[block]))
        leaves.append(made)
        for q in range(PARTS):
            near[q][place[q % 2], block] = made[q * part : (q + 1) * part]

    pl.semaphore_wait(barrier, 2 * (side - 1) + LEVELS - 1 + upper)

    asks = []
    for axis in range(2):
        for step in range(1, side):
            k = axis * (side - 1) + step - 1
            ask = remote(
                partner_ref, wanted.at[axis, place[axis]], ask_send.at[k], ask_recv.at[k],
                (grp, peer(axis, step)[1]),
            )
            ask.start()
            asks.append(ask)
    nears = [[] for _ in range(PARTS)]
    for step in range(1, side):
        for q in range(PARTS):
            mine = near[q].at[place[q % 2]]
            send = remote(
                mine, mine, near_send.at[q, step - 1], near_recv.at[q, step - 1],
                (grp, peer(q % 2, step)[1]),
            )
            send.start()
            nears[q].append(send)

    loads[2].wait()
    whole = [dot(leaves[block], coupling[0, block, 0]) for block in range(blocks)]
    for ask in asks:
        ask.wait_recv()

    def origin(value):
        at = lax.bitwise_and(value, blocks * n_leaf - 1)
        device, block = lax.shift_right_logical(at, blocks.bit_length() - 1), lax.bitwise_and(at, blocks - 1)
        z_bits = side.bit_length() - 1
        return (lax.shift_right_logical(device, z_bits), lax.bitwise_and(device, side - 1)), block

    sources = [origin(partner_ref[block]) for block in range(blocks)]
    asked = [
        [[origin(wanted[axis, peer(axis, step)[0], block]) for block in range(blocks)] for step in range(1, side)]
        for axis in range(2)
    ]

    fars = [[] for _ in range(PARTS)]
    swaps = [[None] * PARTS for _ in range(LEVELS)]
    owns = [[None] * PARTS for _ in range(LEVELS)]

    def pick(q):
        first, second = q % 2, 1 - q % 2
        for send in nears[q]:
            send.wait_recv()
        for step in range(1, side):
            device = peer(second, step)[1]
            for block in range(blocks):
                source, index = asked[second][step - 1][block]
                picked[q, step - 1, block] = near[q][source[first], index]
            send = remote(
                picked.at[q, step - 1], found[q].at[place[second]],
                far_send.at[q, step - 1], far_recv.at[q, step - 1], (grp, device),
            )
            send.start()
            fars[q].append(send)

    def send_level(level, q):
        swap = remote(
            state.at[level, q], other.at[level, q], level_send.at[level, q], level_recv.at[level, q],
            (pairs[level], leaf),
        )
        swap.start()
        swaps[level][q] = swap

    def own_level(level, q):
        owns[level][q] = [
            dot(state[level, q, block], coupling[level + 1, block, 0]) for block in range(blocks)
        ]

    def leaf_step(q):
        for send in fars[q]:
            send.wait_recv()
        for block in range(blocks):
            source, _ = sources[block]
            total = dot(found[q][source[1 - q % 2], block], coupling[0, block, 1])
            state[0, q, block] = keep(1, block, whole[block][q * part : (q + 1) * part] + total)
        send_level(0, q)

    def level_step(level, q):
        swaps[level][q].wait_recv()
        for block in range(blocks):
            total = owns[level][q][block] + dot(other[level, q, block], coupling[level + 1, block, 1])
            state[level + 1, q, block] = keep(level + 2, block, total)
        send_level(level + 1, q)

    def own_last(q):
        owns[LEVELS - 1][q] = [dot(state[LEVELS - 1, q, block], folded[0, block]) for block in range(blocks)]

    def last_step(q):
        here = pl.ds(q * part, part)
        swaps[LEVELS - 1][q].wait_recv()
        for block in range(blocks):
            total = owns[LEVELS - 1][q][block] + dot(other[LEVELS - 1, q, block], folded[1, block])
            out[here, pl.ds(block * size_m, size_m)] = total.astype(jnp.bfloat16)

    for q in range(PARTS):
        pick(q)
    @pl.when(jnp.logical_and(upper == 1, lax.rem(place[1], 2) == 1))
    def _():
        pl.semaphore_signal(answer, inc=1, device_id=(pairs[1], leaf), device_id_type=MESH)

    for q in range(PARTS):
        for block in range(blocks):
            source, index = sources[block]
            found[q][place[1 - q % 2], block] = near[q][source[q % 2], index]
    loads[3].wait()
    width = lax.broadcasted_iota(jnp.int32, (rank, rank), 1)
    for side_of in range(2):
        for block in range(blocks):
            kept = jnp.where(
                width < rank_ref[block, LEVELS + 1], coupling[LEVELS, block, side_of].astype(jnp.float32), 0.0
            ).astype(jnp.bfloat16)
            folded[side_of, block] = dot(kept, expand[block]).astype(jnp.bfloat16)
    for q in range(PARTS):
        leaf_step(q)
    @pl.when(jnp.logical_and(upper == 1, lax.rem(place[1], 2) == 0))
    def _():
        pl.semaphore_signal(answer, inc=1, device_id=(pairs[1], leaf), device_id_type=MESH)

    for q in range(PARTS):
        own_level(0, q)
    pl.when(upper == 0)(lambda: pl.semaphore_wait(answer, 1))
    for q in range(PARTS):
        level_step(0, q)
    for q in range(PARTS):
        own_level(1, q)
    for send in asks + sum(nears + fars, []) + swaps[0]:
        send.wait_send()
    for q in range(PARTS):
        level_step(1, q)
    for q in range(PARTS):
        own_last(q)
    for q in range(PARTS):
        last_step(q)
    for send in swaps[1] + swaps[2]:
        send.wait_send()


def shards(charges, interp_basis, coupling, expand_basis, block_rank, leaf_partner):
    side = math.isqrt(lax.axis_size("leaf"))
    blocks, size_m, rank = interp_basis.shape
    rows = charges.shape[0]
    part = rows // PARTS
    hbm_spec = pl.BlockSpec(memory_space=pltpu.HBM)
    bf16 = jnp.bfloat16
    dma = pltpu.SemaphoreType.DMA
    return pl.pallas_call(
        kernel,
        out_shape=pltpu.VMEM(charges.shape, bf16),
        in_specs=[hbm_spec] * 6,
        out_specs=pl.BlockSpec(memory_space=pltpu.VMEM),
        scratch_shapes=[
            pltpu.VMEM(charges.shape, bf16),
            pltpu.VMEM(interp_basis.shape, bf16),
            pltpu.VMEM(coupling.shape, bf16),
            pltpu.VMEM(expand_basis.shape, bf16),
            pltpu.SMEM(block_rank.shape[::-1], jnp.int32),
            pltpu.SMEM(leaf_partner.shape, jnp.int32),
            pltpu.SMEM((2, side, blocks), jnp.int32),
            pltpu.VMEM((PARTS, side - 1, blocks, part, rank), bf16),
            pltpu.VMEM((LEVELS, PARTS, blocks, part, rank), bf16),
            pltpu.VMEM((LEVELS, PARTS, blocks, part, rank), bf16),
            dma((6,)),
            *[dma((2 * (side - 1),))] * 2,
            *[dma((PARTS, side - 1))] * 4,
            *[dma((LEVELS, PARTS))] * 2,
            pltpu.SemaphoreType.REGULAR,
            pltpu.VMEM((2, blocks, rank, size_m), bf16),
            *[pltpu.VMEM((side, blocks, part, rank), bf16)] * (2 * PARTS),
        ],
        compiler_params=pltpu.CompilerParams(
            collective_id=0, has_side_effects=True, vmem_limit_bytes=60 * 1024 * 1024
        ),
    )(charges, interp_basis, coupling, expand_basis, block_rank.T, leaf_partner)


def solution(mesh):
    in_specs = (
        P(None, ("grp", "leaf")),
        P(("grp", "leaf"), None, None),
        P(None, ("grp", "leaf"), None, None, None),
        P(("grp", "leaf"), None, None),
        P(None, ("grp", "leaf")),
        P(("grp", "leaf")),
    )
    out_specs = P(None, ("grp", "leaf"))
    return jax.shard_map(shards, mesh=mesh, in_specs=in_specs, out_specs=out_specs, check_vma=False)
```
